32 devices in a mesh: section: 4 (over x, core), sample: 2 (over y), tensor: 4 (over z).
Axes of the slice: x: 2, y: 2, z: 4, core: 2. Of those that a mesh axis runs over, the one named last changes fastest.
Arguments:
- queries: bfloat16 [4, 256, 8192], P('section', 'sample', 'tensor'), may hold values from -4.5 to 4.5
- suffix_keys: bfloat16 [4, 256, 1024], P('section', 'sample', 'tensor'), may hold values from -4.5 to 4.5
- suffix_values: bfloat16 [4, 256, 1024], P('section', 'sample', 'tensor'), may hold values from -4.5 to 4.5
- output_grad: bfloat16 [4, 256, 8192], P('section', 'sample', 'tensor'), may hold values from -192 to 192
- prefix_keys: bfloat16 [4, 1024, 1024], P('section', ('sample', 'tensor')), may hold values from -4.5 to 4.5
- prefix_values: bfloat16 [4, 1024, 1024], P('section', ('sample', 'tensor')), may hold values from -4.5 to 4.5
- kv_weight: bfloat16 [4, 8192, 2, 1024], P('section', None, None, 'tensor'), may hold values from -0.0625 to 0.0625
- prefix_states: bfloat16 [4, 1024, 8192], P('section', ('sample', 'tensor')), may hold values from -6 to 6
- norm_gain: bfloat16 [4, 8192], P('section'), may hold values from 0.099609375 to 1.8984375
- segment_ids: int32 [2, 128], P('sample'), may hold values from 0 to 1, never falling along the last dimension, each value on 1 to 96 neighbouring positions
- segment_prompt: int32 [2, 2], P('sample'), may hold values from 0 to 2
- block_table: int32 [3, 4], replicated, may hold values from 0 to 7, as said below
Outputs:
- query_grad: bfloat16 [4, 256, 8192], P('section', 'sample', 'tensor')
- rollout_key_gradient: bfloat16 [4, 256, 1024], P('section', 'sample', 'tensor')
- suffix_value_grad: bfloat16 [4, 256, 1024], P('section', 'sample', 'tensor')
- prefix_key_grad: float32 [4, 1024, 1024], P('section', ('sample', 'tensor'))
- prefix_value_grad: float32 [4, 1024, 1024], P('section', ('sample', 'tensor'))
- prefix_state_gradient: float32 [4, 1024, 8192], P('section', ('sample', 'tensor'))
The draws below stay inside these ranges and needn't reach their ends.
Inputs may be any that keep to these rules, and one draw needn't show every extreme that they name: `block_table`: each row lists 4 distinct pages; its first 2 entries are the same pages in every row, and every page of the pool appears in some row.
All inputs are finite; a program needn't handle non-finite values.
Results may differ from the reference program's by a relative error of at most 0.024.
Values may be sent and summed in bfloat16 or wider, within the bound.
A program may use at most 192 MiB of HBM per device.

```python
import math
import jax
import jax.numpy as jnp
import numpy as np
from jax import lax

D = 8192
QH = 64
KEY_VALUE_HEADS = 8
HEAD_SIZE = 128
PAGE = 128
SEG_DEV = 2
NPROMPT = 3
TOK_DEV = 128
LAYERS = 4
HEAD_GROUPS = 4
ROW_BLOCKS = 2
ROLLOUT_TOKENS = 256
NPAGES = 8
PREFIX_POOL_ROWS = 1024


def page_order(key):
    return jax.random.permutation(jax.random.fold_in(key, 11), NPAGES).astype(jnp.int32)


def draw_block_table(key, part):
    page_perm = page_order(key)
    shared = NPAGES // 4
    table_rows = []
    for prompt in range(NPROMPT):
        own_pages = page_perm[shared * (1 + prompt):shared * (2 + prompt)]
        table_rows.append(jnp.concatenate([page_perm[:shared], own_pages]))
    return jnp.stack(table_rows).astype(jnp.int32)


def draw_prefix_keys(key, part):
    base_key = jax.random.fold_in(key, 13)
    key_draw = jnp.clip(jax.random.normal(base_key, (LAYERS, PREFIX_POOL_ROWS, KEY_VALUE_HEADS * HEAD_SIZE), jnp.float32), -4.5, 4.5)
    return key_draw.astype(jnp.bfloat16)


def draw_queries(key, part):
    base_key = jax.random.fold_in(key, 14)
    query_draw = jnp.clip(jax.random.normal(base_key, (LAYERS, ROLLOUT_TOKENS, QH * HEAD_SIZE), jnp.float32), -4.5, 4.5)
    return query_draw.astype(jnp.bfloat16)


def touch_ends(result, own_key, least, largest):
    index_at = [jax.random.randint(jax.random.fold_in(own_key, axis), (), 0, length) for axis, length in enumerate(result.shape)]
    longest = result.shape.index(max(result.shape))
    next_to = index_at[:longest] + [(index_at[longest] + 1) % result.shape[longest]] + index_at[longest + 1:]
    return result.at[tuple(index_at)].set(least).at[tuple(next_to)].set(largest)


def shard_levels(key, extent, split, least, high):
    def one(dim, shards_of):
        heights = jax.random.uniform(jax.random.fold_in(jax.random.fold_in(key, 6), dim), (shards_of,), jnp.float32, least / len(split), high / len(split))
        return jnp.repeat(jnp.exp(heights), extent[dim] // shards_of).reshape((-1,) + (1,) * (len(extent) - dim - 1))

    gain = one(*split[0])
    for cut in split[1:]:
        gain = gain * one(*cut)
    return gain


def split_up(number_of, total, reach, slope):
    portions = [(1 << 20) // math.isqrt(standing ** slope) + 1 for standing in range(2, number_of + 1)]
    rest, holding = total - reach - (number_of - 1), [1] * (number_of - 1)
    while rest > 0:
        free = [i for i in range(number_of - 1) if holding[i] < reach]
        pool, left = sum([portions[i] for i in free]), rest
        for i in free:
            addition = min(reach - holding[i], max(1, left * portions[i] // pool), rest)
            holding[i] = holding[i] + addition
            rest = rest - addition
    return np.array([reach] + holding)


def uneven_parts(stream_key, number_of, total, limit, lean):
    if number_of == 2:
        one = jax.random.randint(stream_key, (), max(1, total - limit), min(limit, total - 1) + 1)
        return jnp.stack([one, total - one])
    sizes = jnp.asarray(split_up(number_of, total, limit, lean), jnp.int32)
    twos = (number_of - 1) // 2
    giver, receiver = sizes[1:1 + 2 * twos:2], sizes[2:2 + 2 * twos:2]
    slack = jnp.minimum(giver - 1, limit - receiver)
    shifted = jax.random.randint(jax.random.fold_in(stream_key, 1), (twos,), 0, 1 << 20) % (slack + 1)
    sizes = sizes.at[1:1 + 2 * twos:2].set(giver - shifted).at[2:2 + 2 * twos:2].set(receiver + shifted)
    return sizes[jax.random.permutation(jax.random.fold_in(stream_key, 2), number_of)]


def scatter_about(rng, dims, deviation, reach, shards=(), kind=jnp.bfloat16):
    loudness = shard_levels(rng, dims, shards, -0.22, 0.18) if shards else 1.0
    result = jax.random.normal(rng, dims, jnp.float32) * deviation * loudness
    return jnp.minimum(jnp.maximum(result, -reach), reach).astype(kind)


def setup_inputs(seed: int = 0) -> dict:
    keys = jax.random.split(jax.random.key(seed), 13)
    queries = draw_queries(jax.random.fold_in(keys[12], 71), 0)
    suffix_keys = scatter_about(keys[1], (LAYERS, ROLLOUT_TOKENS, KEY_VALUE_HEADS * HEAD_SIZE), 1.0, 4.5, ((0, 4), (1, 2), (2, 4)))
    suffix_values = scatter_about(keys[2], (LAYERS, ROLLOUT_TOKENS, KEY_VALUE_HEADS * HEAD_SIZE), 1.0, 4.5, ((0, 4), (1, 2), (2, 4)))
    output_grad = scatter_about(keys[3], (LAYERS, ROLLOUT_TOKENS, QH * HEAD_SIZE), 32.0, 192.0, ((0, 4), (1, 2), (2, 4)))
    prefix_keys = draw_prefix_keys(jax.random.fold_in(keys[12], 71), 0)
    prefix_values = scatter_about(keys[5], (LAYERS, PREFIX_POOL_ROWS, KEY_VALUE_HEADS * HEAD_SIZE), 1.0, 4.5, ((0, 4), (1, 8)))
    kv_weight = scatter_about(keys[6], (LAYERS, D, 2, KEY_VALUE_HEADS * HEAD_SIZE), D ** -0.5, 0.0625, ((0, 4), (3, 4)))
    prefix_states = scatter_about(keys[7], (LAYERS, PREFIX_POOL_ROWS, D), 1.0, 6.0, ((0, 4), (1, 8)))
    norm_gain = jnp.clip(1.0 + 0.18 * jax.random.normal(keys[8], (LAYERS, D), jnp.float32), 0.099609375, 1.8984375).astype(jnp.bfloat16)
    segment_ids = jax.vmap(lambda own: jnp.searchsorted(jnp.cumsum(uneven_parts(own, SEG_DEV, TOK_DEV, 3 * TOK_DEV // 4, 1)), jnp.arange(TOK_DEV), side="right"))(jax.random.split(keys[9], ROW_BLOCKS)).reshape((ROW_BLOCKS, TOK_DEV)).astype(jnp.int32)
    segment_prompt = touch_ends(jax.random.randint(keys[10], (ROW_BLOCKS, SEG_DEV), 0, NPROMPT), jax.random.fold_in(keys[10], 1), 0, NPROMPT - 1).astype(jnp.int32)
    block_table = draw_block_table(jax.random.fold_in(keys[12], 71), 0)
    return dict(queries=queries, suffix_keys=suffix_keys, suffix_values=suffix_values, output_grad=output_grad, prefix_keys=prefix_keys, prefix_values=prefix_values, kv_weight=kv_weight, prefix_states=prefix_states, norm_gain=norm_gain, segment_ids=segment_ids, segment_prompt=segment_prompt, block_table=block_table)


MASKED_SCORE = -1e+30
EPSILON = 1e-05

def visible_keys(seg_row, prompt_row, table, pooled_rows):
    tok_count = seg_row.shape[0]
    seg_hot = seg_row[:, None] == jnp.arange(prompt_row.shape[0], dtype=jnp.int32)[None, :]
    prompt_tok = lax.optimization_barrier(jnp.sum(jnp.where(seg_hot, prompt_row[None, :], 0), axis=1)).astype(jnp.int32)
    page_ids = jnp.arange(pooled_rows // PAGE, dtype=jnp.int32)
    member = jnp.any(table[:, :, None] == page_ids[None, None, :], axis=1)
    prompt_hot = prompt_tok[:, None] == jnp.arange(table.shape[0], dtype=jnp.int32)[None, :]
    member_tok = jnp.any(prompt_hot[:, :, None] & member[None, :, :], axis=1)
    prefix_seen = jnp.repeat(member_tok, PAGE, axis=1)
    position = jnp.arange(tok_count, dtype=jnp.int32)
    suffix_seen = (seg_row[:, None] == seg_row[None, :]) & (position[None, :] <= position[:, None])
    return jnp.concatenate([prefix_seen, suffix_seen], axis=1)

def attend_group(query_grp, grad_grp, key_rows, value_rows, visible):
    inv_root = query_grp.shape[-1] ** (-0.5)
    query_wide = query_grp.astype(jnp.float32)
    grad_wide = grad_grp.astype(jnp.float32)
    key_wide = key_rows.astype(jnp.float32)
    value_wide = value_rows.astype(jnp.float32)
    scores = jnp.einsum('rgd,kd->rgk', query_wide, key_wide) * inv_root
    scores = jnp.where(visible[:, None, :], scores, MASKED_SCORE)
    row_max = lax.optimization_barrier(jnp.max(scores, axis=2, keepdims=True))
    exponent = jnp.exp(scores - row_max)
    softmax_w = exponent / lax.optimization_barrier(jnp.sum(exponent, axis=2, keepdims=True))
    weights_low = softmax_w.astype(jnp.bfloat16).astype(jnp.float32)
    attended = jnp.einsum('rgk,kd->rgd', weights_low, value_wide)
    delta_row = lax.optimization_barrier(jnp.sum(grad_wide * attended, axis=2, keepdims=True))
    weight_grad = jnp.einsum('rgd,kd->rgk', grad_wide, value_wide)
    score_grad = (softmax_w * (weight_grad - delta_row)).astype(jnp.bfloat16).astype(jnp.float32)
    query_out = jnp.einsum('rgk,kd->rgd', score_grad, key_wide) * inv_root
    key_result = jnp.einsum('rgk,rgd->kd', score_grad, query_wide) * inv_root
    value_out = jnp.einsum('rgk,rgd->kd', weights_low, grad_wide)
    return (query_out, key_result, value_out)

def reference(queries, suffix_keys, suffix_values, output_grad, prefix_keys, prefix_values, kv_weight, prefix_states, norm_gain, segment_ids, segment_prompt, block_table):
    group_size = QH // KEY_VALUE_HEADS
    col_width = KEY_VALUE_HEADS * HEAD_SIZE // HEAD_GROUPS
    query_full, suffix_key_full, suffix_value_full, prefix_key_full, prefix_value_full, term_list = ([], [], [], [], [], [])
    for layer_idx in range(LAYERS):
        key_pool = prefix_keys[layer_idx]
        value_pool = prefix_values[layer_idx]

        def single_block(carry, block_args):
            query_b, grad_b, key_b, value_b, seg_row, prompt_row = block_args
            visible = visible_keys(seg_row, prompt_row, block_table, PREFIX_POOL_ROWS)
            query_h = query_b.reshape(TOK_DEV, KEY_VALUE_HEADS, group_size, HEAD_SIZE)
            grad_h = grad_b.reshape(TOK_DEV, KEY_VALUE_HEADS, group_size, HEAD_SIZE)
            query_pieces, suffix_key_pieces, suffix_value_pieces, prefix_key_pieces, prefix_value_pieces = ([], [], [], [], [])
            for head_index in range(KEY_VALUE_HEADS):
                col_range = slice(head_index * HEAD_SIZE, (head_index + 1) * HEAD_SIZE)
                key_rows = jnp.concatenate([key_pool[:, col_range], key_b[:, col_range]], axis=0)
                value_rows = jnp.concatenate([value_pool[:, col_range], value_b[:, col_range]], axis=0)
                query_out, key_result, value_out = attend_group(query_h[:, head_index], grad_h[:, head_index], key_rows, value_rows, visible)
                query_pieces.append(query_out)
                prefix_key_pieces.append(key_result[:PREFIX_POOL_ROWS])
                suffix_key_pieces.append(key_result[PREFIX_POOL_ROWS:])
                prefix_value_pieces.append(value_out[:PREFIX_POOL_ROWS])
                suffix_value_pieces.append(value_out[PREFIX_POOL_ROWS:])
            query_grad_block = jnp.stack(query_pieces, axis=1).reshape(TOK_DEV, QH * HEAD_SIZE).astype(jnp.bfloat16)
            suffix_key_block = jnp.concatenate(suffix_key_pieces, axis=1).astype(jnp.bfloat16)
            suffix_value_block = jnp.concatenate(suffix_value_pieces, axis=1).astype(jnp.bfloat16)
            next_carry = (carry[0] + jnp.concatenate(prefix_key_pieces, axis=1), carry[1] + jnp.concatenate(prefix_value_pieces, axis=1))
            return (next_carry, (query_grad_block, suffix_key_block, suffix_value_block))
        block_list = (queries[layer_idx].reshape(ROW_BLOCKS, TOK_DEV, QH * HEAD_SIZE), output_grad[layer_idx].reshape(ROW_BLOCKS, TOK_DEV, QH * HEAD_SIZE), suffix_keys[layer_idx].reshape(ROW_BLOCKS, TOK_DEV, KEY_VALUE_HEADS * HEAD_SIZE), suffix_values[layer_idx].reshape(ROW_BLOCKS, TOK_DEV, KEY_VALUE_HEADS * HEAD_SIZE), segment_ids, segment_prompt)
        empty_sums = (jnp.zeros((PREFIX_POOL_ROWS, KEY_VALUE_HEADS * HEAD_SIZE), jnp.float32), jnp.zeros((PREFIX_POOL_ROWS, KEY_VALUE_HEADS * HEAD_SIZE), jnp.float32))
        (pooled_key, pooled_value), (query_grad_layer, suffix_key_layer, suffix_value_layer) = lax.scan(single_block, empty_sums, block_list)
        query_full.append(query_grad_layer.reshape(ROLLOUT_TOKENS, QH * HEAD_SIZE))
        suffix_key_full.append(suffix_key_layer.reshape(ROLLOUT_TOKENS, KEY_VALUE_HEADS * HEAD_SIZE))
        suffix_value_full.append(suffix_value_layer.reshape(ROLLOUT_TOKENS, KEY_VALUE_HEADS * HEAD_SIZE))
        prefix_key_full.append(pooled_key)
        prefix_value_full.append(pooled_value)
        key_low = pooled_key.astype(jnp.bfloat16)
        value_low = pooled_value.astype(jnp.bfloat16)
        normed_grad = jnp.zeros((PREFIX_POOL_ROWS, D), jnp.float32)
        for group_idx in range(HEAD_GROUPS):
            col_range = slice(group_idx * col_width, (group_idx + 1) * col_width)
            grad_cols = jnp.concatenate([key_low[:, col_range], value_low[:, col_range]], axis=1)
            weight_cols = jnp.concatenate([kv_weight[layer_idx, :, 0, col_range], kv_weight[layer_idx, :, 1, col_range]], axis=1)
            group_term = lax.optimization_barrier(jnp.dot(grad_cols, weight_cols.T, preferred_element_type=jnp.float32).astype(jnp.bfloat16))
            normed_grad = normed_grad + group_term.astype(jnp.float32)
        states = prefix_states[layer_idx].astype(jnp.float32)
        gain_wide = norm_gain[layer_idx].astype(jnp.float32)[None, :]
        inv_rms = lax.rsqrt(lax.optimization_barrier(jnp.mean(states * states, axis=1, keepdims=True)) + EPSILON)
        gained = gain_wide * normed_grad
        layer_term = inv_rms * gained - states * inv_rms ** 3 * lax.optimization_barrier(jnp.mean(states * gained, axis=1, keepdims=True))
        term_list.append(layer_term)
    stacked_terms = jnp.stack(term_list, axis=0)
    prefix_state_gradient = jnp.flip(jnp.cumsum(jnp.flip(stacked_terms, 0), axis=0), 0)
    return (jnp.stack(query_full, 0), jnp.stack(suffix_key_full, 0), jnp.stack(suffix_value_full, 0), jnp.stack(prefix_key_full, 0), jnp.stack(prefix_value_full, 0), prefix_state_gradient)
```

```python
import jax
import jax.numpy as jnp
from jax import lax
from jax.sharding import PartitionSpec as P

HEAD_SIZE = 128
PAGE = 128


MASKED_SCORE = -1e30
EPSILON = 1e-05
CHUNKS = 4
AHEAD = 2


def visible_keys(seg_row, prompt_row, table, page_ids):
    tok_count = seg_row.shape[0]
    seg_hot = seg_row[:, None] == jnp.arange(prompt_row.shape[0], dtype=jnp.int32)[None, :]
    prompt_tok = jnp.sum(jnp.where(seg_hot, prompt_row[None, :], 0), axis=1)
    member = jnp.any(table[:, :, None] == page_ids[None, None, :], axis=1)
    prompt_hot = prompt_tok[:, None] == jnp.arange(table.shape[0], dtype=jnp.int32)[None, :]
    member_tok = jnp.any(prompt_hot[:, :, None] & member[None, :, :], axis=1)
    prefix_seen = jnp.repeat(member_tok, PAGE, axis=1)
    position = jnp.arange(tok_count, dtype=jnp.int32)
    suffix_seen = (seg_row[:, None] == seg_row[None, :]) & (position[None, :] <= position[:, None])
    return jnp.concatenate([prefix_seen, suffix_seen], axis=1)


def attend_group(query_grp, grad_grp, key_rows, value_rows, visible):
    inv_root = query_grp.shape[-1] ** (-0.5)
    scores = (
        jnp.einsum("rgd,kd->rgk", query_grp, key_rows, preferred_element_type=jnp.float32)
        * inv_root
    )
    scores = jnp.where(visible[:, None, :], scores, MASKED_SCORE)
    row_max = jnp.max(scores, axis=2, keepdims=True)
    exponent = jnp.exp(scores - row_max)
    softmax_w = exponent / jnp.sum(exponent, axis=2, keepdims=True)
    weights_low = softmax_w.astype(jnp.bfloat16)
    attended = jnp.einsum(
        "rgk,kd->rgd", weights_low, value_rows, preferred_element_type=jnp.float32
    )
    delta_row = jnp.sum(grad_grp.astype(jnp.float32) * attended, axis=2, keepdims=True)
    weight_grad = jnp.einsum(
        "rgd,kd->rgk", grad_grp, value_rows, preferred_element_type=jnp.float32
    )
    score_grad = (softmax_w * (weight_grad - delta_row)).astype(jnp.bfloat16)
    query_out = (
        jnp.einsum("rgk,kd->rgd", score_grad, key_rows, preferred_element_type=jnp.float32)
        * inv_root
    )
    key_result = (
        jnp.einsum("rgk,rgd->kd", score_grad, query_grp, preferred_element_type=jnp.float32)
        * inv_root
    )
    value_out = jnp.einsum("rgk,rgd->kd", weights_low, grad_grp, preferred_element_type=jnp.float32)
    return (query_out, key_result, value_out)


def swap(value, axis, bit):
    count = lax.axis_size(axis)
    return lax.ppermute(value, axis, [(i, i ^ bit) for i in range(count)])


def sample_gather(value, axis):
    if lax.axis_size("sample") == 2:
        return jnp.concatenate([value, swap(value, "sample", 1)], axis=axis)
    return lax.all_gather(value, "sample", axis=axis, tiled=True)


def sample_reduce(value):
    count = lax.axis_size("sample")
    rows = value.shape[0] // count
    if count == 2:
        theirs = swap(value[rows:].astype(jnp.bfloat16), "sample", 1)
        return value[:rows] + theirs.astype(jnp.float32)
    low = value.astype(jnp.bfloat16)
    return lax.psum_scatter(low, "sample", scatter_dimension=0, tiled=True).astype(jnp.float32)


def times_weight(rows, weight):
    return lax.dot_general(
        rows, weight, (((rows.ndim - 1,), (1,)), ((), ())), preferred_element_type=jnp.float32
    )


def suffix_sum(term):
    count = lax.axis_size("section")
    place = lax.axis_index("section")
    low = term.astype(jnp.bfloat16)
    if count != 4:
        gathered = lax.all_gather(low, "section").astype(jnp.float32)
        above = (jnp.arange(count) > place)[:, None, None]
        return term + jnp.sum(jnp.where(above, gathered, 0.0), axis=0)
    odd = place % 2 == 1
    half = term.shape[1] // 2
    peer = swap(low, "section", 1).astype(jnp.float32)
    pair = (term + peer).astype(jnp.bfloat16)
    part = jnp.where(odd, pair[:, half:], pair[:, :half])
    got = lax.ppermute(part, "section", [(2, 0), (3, 1)])
    other = lax.ppermute(got, "section", [(0, 1), (1, 0)])
    upper = jnp.where(
        odd, jnp.concatenate([other, got], axis=1), jnp.concatenate([got, other], axis=1)
    )
    return term + jnp.where(odd, 0.0, peer) + upper.astype(jnp.float32)


def from_above(value, step):
    count = lax.axis_size("section")
    return lax.ppermute(value, "section", [(i, i - step) for i in range(step, count)])


def on_device(
    queries,
    suffix_keys,
    suffix_values,
    output_grad,
    prefix_keys,
    prefix_values,
    kv_weight,
    prefix_states,
    norm_gain,
    segment_ids,
    segment_prompt,
    block_table,
):
    head_width = suffix_keys.shape[2]
    samples = lax.axis_size("sample")
    sample = lax.axis_index("sample")
    tensors = lax.axis_size("tensor")
    tensor = lax.axis_index("tensor")
    sections = lax.axis_size("section")

    pool_own = jnp.concatenate([prefix_keys, prefix_values], axis=0)
    pool_mine = lax.all_to_all(pool_own, "tensor", split_axis=2, concat_axis=1, tiled=True)
    pool = sample_gather(pool_mine, 1)
    key_pool, value_pool = pool[0], pool[1]
    pooled_rows = key_pool.shape[0]
    pages = pooled_rows // PAGE
    page_ids = jnp.arange(pages, dtype=jnp.int32)
    if samples == 2:
        page_ids = (page_ids + sample.astype(jnp.int32) * (pages // 2)) % pages

    weight = kv_weight[0].reshape(kv_weight.shape[1], 2 * head_width)
    width = weight.shape[0]
    step = width // CHUNKS
    piece = step // samples
    weight_tied, pool_mine = lax.optimization_barrier((weight, pool_mine))
    partner_weight = []
    for chunk in range(AHEAD):
        mine = lax.dynamic_slice_in_dim(weight_tied, chunk * step + sample * piece, piece, 0)
        partner_weight.append(sample_gather(swap(mine, "tensor", 1), 0))

    states_low = prefix_states[0]
    states_tied, pool_mine = lax.optimization_barrier((states_low, pool_mine))
    states_above = [from_above(states_tied, hop) for hop in range(1, sections)]

    tok_count = queries.shape[1]
    kv_local = head_width // HEAD_SIZE
    group_size = queries.shape[2] // head_width
    visible = visible_keys(segment_ids[0], segment_prompt[0], block_table, page_ids)
    query_rows = queries[0].reshape(tok_count, kv_local, group_size, HEAD_SIZE)
    grad_rows = output_grad[0].reshape(tok_count, kv_local, group_size, HEAD_SIZE)
    own_keys = suffix_keys[0]
    own_values = suffix_values[0]
    query_pieces, suffix_key_pieces, suffix_value_pieces, prefix_key_pieces, prefix_value_pieces = (
        [],
        [],
        [],
        [],
        [],
    )
    for head_index in range(kv_local):
        low_col = head_index * HEAD_SIZE
        cols = slice(low_col, low_col + HEAD_SIZE)
        key_rows = jnp.concatenate([key_pool[:, cols], own_keys[:, cols]], axis=0)
        value_rows = jnp.concatenate([value_pool[:, cols], own_values[:, cols]], axis=0)
        query_out, key_result, value_out = attend_group(
            query_rows[:, head_index], grad_rows[:, head_index], key_rows, value_rows, visible
        )
        query_pieces.append(query_out)
        prefix_key_pieces.append(key_result[:pooled_rows])
        suffix_key_pieces.append(key_result[pooled_rows:])
        prefix_value_pieces.append(value_out[:pooled_rows])
        suffix_value_pieces.append(value_out[pooled_rows:])
    query_grad = jnp.stack(query_pieces, axis=1).reshape(tok_count, -1).astype(jnp.bfloat16)
    rollout_key_gradient = jnp.concatenate(suffix_key_pieces, axis=1).astype(jnp.bfloat16)
    suffix_value_grad = jnp.concatenate(suffix_value_pieces, axis=1).astype(jnp.bfloat16)
    pooled = jnp.concatenate(prefix_key_pieces + prefix_value_pieces, axis=1)
    reduced = sample_reduce(pooled).astype(jnp.bfloat16)

    own_rows = reduced.shape[0] // tensors
    high, low = tensor // 2, tensor % 2
    by_owner = reduced.reshape(tensors // 2, 2, own_rows, 2 * head_width)
    keep = lax.dynamic_index_in_dim(by_owner, low, 1, False)
    give = lax.dynamic_index_in_dim(by_owner, 1 - low, 1, False)
    partner = swap(give, "tensor", 1)
    here = lambda rows: lax.dynamic_index_in_dim(rows, high, 0, False)
    there = lambda rows: lax.dynamic_index_in_dim(rows, 1 - high, 0, False)

    gain_wide = norm_gain[0].astype(jnp.float32)[None, :]
    states = states_low.astype(jnp.float32)
    inv_rms = lax.rsqrt(jnp.mean(states * states, axis=1, keepdims=True) + EPSILON)

    def partner_product(rows, chunk):
        pieces = times_weight(rows, partner_weight[chunk])
        if samples != 2:
            return pieces
        turned = jnp.concatenate([pieces[:, piece:], pieces[:, :piece]], axis=1)
        return jnp.where(sample == 0, pieces, turned)

    local, sent = {}, {}
    for chunk in range(AHEAD):
        own = weight[chunk * step : (chunk + 1) * step]
        total = times_weight(there(keep), own) + partner_product(there(partner), chunk)
        sent[chunk] = swap(total.astype(jnp.bfloat16), "tensor", 2)
        local[chunk] = times_weight(here(keep), own) + partner_product(here(partner), chunk)
    for chunk in range(AHEAD, CHUNKS):
        own = weight[chunk * step : (chunk + 1) * step]
        theirs = swap(times_weight(give, own).astype(jnp.bfloat16), "tensor", 1)
        total = times_weight(there(keep), own) + there(theirs).astype(jnp.float32)
        sent[chunk] = swap(total.astype(jnp.bfloat16), "tensor", 2)
        local[chunk] = times_weight(here(keep), own) + here(theirs).astype(jnp.float32)

    sums, along = [], 0.0
    for chunk in range(CHUNKS):
        cols = slice(chunk * step, (chunk + 1) * step)
        normed = local[chunk] + sent[chunk].astype(jnp.float32)
        gained = gain_wide[:, cols] * normed
        along = along + jnp.sum(states[:, cols] * gained, axis=1)
        sums.append(suffix_sum(inv_rms * gained))
    slope = inv_rms[:, 0] ** 3 * (along / width)
    state_part = states * slope[:, None]
    for hop in range(1, sections):
        slope_above = from_above(slope, hop)
        state_part = state_part + states_above[hop - 1].astype(jnp.float32) * slope_above[:, None]
    prefix_state_gradient = jnp.concatenate(sums, axis=1) - state_part

    home = lax.all_to_all(
        reduced.reshape(-1, 2, head_width), "tensor", split_axis=0, concat_axis=2, tiled=True
    ).astype(jnp.float32)
    return (
        query_grad[None],
        rollout_key_gradient[None],
        suffix_value_grad[None],
        home[:, 0][None],
        home[:, 1][None],
        prefix_state_gradient[None],
    )


def solution(mesh):
    placed = (
        P("section", "sample", "tensor"),
        P("section", "sample", "tensor"),
        P("section", "sample", "tensor"),
        P("section", "sample", "tensor"),
        P("section", ("sample", "tensor"), None),
        P("section", ("sample", "tensor"), None),
        P("section", None, None, "tensor"),
        P("section", ("sample", "tensor"), None),
        P("section", None),
        P("sample", None),
        P("sample", None),
        P(),
    )
    return jax.shard_map(
        on_device,
        mesh=mesh,
        in_specs=placed,
        out_specs=(
            P("section", "sample", "tensor"),
            P("section", "sample", "tensor"),
            P("section", "sample", "tensor"),
            P("section", ("sample", "tensor"), None),
            P("section", ("sample", "tensor"), None),
            P("section", ("sample", "tensor"), None),
        ),
        check_vma=False,
    )
```

```python
import jax
import jax.numpy as jnp
from jax import lax
from jax.sharding import PartitionSpec as P

HEAD_SIZE = 128
PAGE = 128


MASKED_SCORE = -1e30
EPSILON = 1e-05
CHUNKS = 4
AHEAD = 2


def visible_keys(seg_row, prompt_row, table, page_ids):
    tok_count = seg_row.shape[0]
    seg_hot = seg_row[:, None] == jnp.arange(prompt_row.shape[0], dtype=jnp.int32)[None, :]
    prompt_tok = jnp.sum(jnp.where(seg_hot, prompt_row[None, :], 0), axis=1)
    member = jnp.any(table[:, :, None] == page_ids[None, None, :], axis=1)
    prompt_hot = prompt_tok[:, None] == jnp.arange(table.shape[0], dtype=jnp.int32)[None, :]
    member_tok = jnp.any(prompt_hot[:, :, None] & member[None, :, :], axis=1)
    prefix_seen = jnp.repeat(member_tok, PAGE, axis=1)
    position = jnp.arange(tok_count, dtype=jnp.int32)
    suffix_seen = (seg_row[:, None] == seg_row[None, :]) & (position[None, :] <= position[:, None])
    return jnp.concatenate([prefix_seen, suffix_seen], axis=1)


def attend_group(query_grp, grad_grp, key_rows, value_rows, visible):
    inv_root = query_grp.shape[-1] ** (-0.5)
    scores = (
        jnp.einsum("rgd,kd->rgk", query_grp, key_rows, preferred_element_type=jnp.float32)
        * inv_root
    )
    scores = jnp.where(visible[:, None, :], scores, MASKED_SCORE)
    row_max = jnp.max(scores, axis=2, keepdims=True)
    exponent = jnp.exp(scores - row_max)
    softmax_w = exponent / jnp.sum(exponent, axis=2, keepdims=True)
    weights_low = softmax_w.astype(jnp.bfloat16)
    attended = jnp.einsum(
        "rgk,kd->rgd", weights_low, value_rows, preferred_element_type=jnp.float32
    )
    delta_row = jnp.sum(grad_grp.astype(jnp.float32) * attended, axis=2, keepdims=True)
    weight_grad = jnp.einsum(
        "rgd,kd->rgk", grad_grp, value_rows, preferred_element_type=jnp.float32
    )
    score_grad = (softmax_w * (weight_grad - delta_row)).astype(jnp.bfloat16)
    query_out = (
        jnp.einsum("rgk,kd->rgd", score_grad, key_rows, preferred_element_type=jnp.float32)
        * inv_root
    )
    key_result = (
        jnp.einsum("rgk,rgd->kd", score_grad, query_grp, preferred_element_type=jnp.float32)
        * inv_root
    )
    value_out = jnp.einsum("rgk,rgd->kd", weights_low, grad_grp, preferred_element_type=jnp.float32)
    return (query_out, key_result, value_out)


def swap(value, axis, bit):
    count = lax.axis_size(axis)
    return lax.ppermute(value, axis, [(i, i ^ bit) for i in range(count)])


def sample_gather(value, axis):
    if lax.axis_size("sample") == 2:
        return jnp.concatenate([value, swap(value, "sample", 1)], axis=axis)
    return lax.all_gather(value, "sample", axis=axis, tiled=True)


def sample_reduce(value):
    count = lax.axis_size("sample")
    rows = value.shape[0] // count
    if count == 2:
        theirs = swap(value[rows:].astype(jnp.bfloat16), "sample", 1)
        return value[:rows] + theirs.astype(jnp.float32)
    low = value.astype(jnp.bfloat16)
    return lax.psum_scatter(low, "sample", scatter_dimension=0, tiled=True).astype(jnp.float32)


def times_weight(rows, weight):
    last = rows.ndim - 1
    return lax.dot_general(
        rows, weight, (((last - 1, last), (1, 2)), ((), ())), preferred_element_type=jnp.float32
    )


def tied(*values):
    return lax.optimization_barrier(values)


def suffix_sum(term):
    count = lax.axis_size("section")
    place = lax.axis_index("section")
    low = term.astype(jnp.bfloat16)
    if count != 4:
        gathered = lax.all_gather(low, "section").astype(jnp.float32)
        above = (jnp.arange(count) > place)[:, None, None]
        return term + jnp.sum(jnp.where(above, gathered, 0.0), axis=0)
    odd = place % 2 == 1
    half = term.shape[1] // 2
    peer = swap(low, "section", 1).astype(jnp.float32)
    pair = (term + peer).astype(jnp.bfloat16)
    part = jnp.where(odd, pair[:, half:], pair[:, :half])
    got = lax.ppermute(part, "section", [(2, 0), (3, 1)])
    other = lax.ppermute(got, "section", [(0, 1), (1, 0)])
    upper = jnp.where(
        odd, jnp.concatenate([other, got], axis=1), jnp.concatenate([got, other], axis=1)
    )
    return term + jnp.where(odd, 0.0, peer) + upper.astype(jnp.float32)


def from_above(value, step):
    count = lax.axis_size("section")
    return lax.ppermute(value, "section", [(i, i - step) for i in range(step, count)])


def on_device(
    queries,
    suffix_keys,
    suffix_values,
    output_grad,
    prefix_keys,
    prefix_values,
    kv_weight,
    prefix_states,
    norm_gain,
    segment_ids,
    segment_prompt,
    block_table,
):
    head_width = suffix_keys.shape[2]
    samples = lax.axis_size("sample")
    sample = lax.axis_index("sample")
    tensors = lax.axis_size("tensor")
    tensor = lax.axis_index("tensor")
    sections = lax.axis_size("section")

    pool_own = jnp.concatenate([prefix_keys, prefix_values], axis=0)
    pool_mine = lax.all_to_all(pool_own, "tensor", split_axis=2, concat_axis=1, tiled=True)
    pool = sample_gather(pool_mine, 1)
    key_pool, value_pool = pool[0], pool[1]
    pooled_rows = key_pool.shape[0]
    pages = pooled_rows // PAGE
    page_ids = jnp.arange(pages, dtype=jnp.int32)
    if samples == 2:
        page_ids = (page_ids + sample.astype(jnp.int32) * (pages // 2)) % pages

    weight = kv_weight[0]
    width = weight.shape[0]
    step = width // CHUNKS
    piece = step // samples
    partner_half = []
    for chunk in range(AHEAD):
        mine = lax.dynamic_slice_in_dim(weight, chunk * step + sample * piece, piece, 0)
        partner_half.append(swap(mine, "tensor", 1))

    states_low = prefix_states[0]
    if sections == 4:
        states_across = [lax.ppermute(states_low, "section", [(2, 0), (3, 1)])]
    else:
        states_across = [from_above(states_low, hop) for hop in range(1, sections)]

    tok_count = queries.shape[1]
    kv_local = head_width // HEAD_SIZE
    group_size = queries.shape[2] // head_width
    visible = visible_keys(segment_ids[0], segment_prompt[0], block_table, page_ids)
    query_rows = queries[0].reshape(tok_count, kv_local, group_size, HEAD_SIZE)
    grad_rows = output_grad[0].reshape(tok_count, kv_local, group_size, HEAD_SIZE)
    own_keys = suffix_keys[0]
    own_values = suffix_values[0]
    query_pieces, suffix_key_pieces, suffix_value_pieces, prefix_key_pieces, prefix_value_pieces = (
        [],
        [],
        [],
        [],
        [],
    )
    for head_index in range(kv_local):
        low_col = head_index * HEAD_SIZE
        cols = slice(low_col, low_col + HEAD_SIZE)
        if head_index == 1:
            key_pool, value_pool, partner_half, states_across = tied(
                key_pool, value_pool, partner_half, states_across
            )
        key_rows = jnp.concatenate([key_pool[:, cols], own_keys[:, cols]], axis=0)
        value_rows = jnp.concatenate([value_pool[:, cols], own_values[:, cols]], axis=0)
        query_out, key_result, value_out = attend_group(
            query_rows[:, head_index], grad_rows[:, head_index], key_rows, value_rows, visible
        )
        query_pieces.append(query_out)
        prefix_key_pieces.append(key_result[:pooled_rows])
        suffix_key_pieces.append(key_result[pooled_rows:])
        prefix_value_pieces.append(value_out[:pooled_rows])
        suffix_value_pieces.append(value_out[pooled_rows:])
    query_grad = jnp.stack(query_pieces, axis=1).reshape(tok_count, -1).astype(jnp.bfloat16)
    rollout_key_gradient = jnp.concatenate(suffix_key_pieces, axis=1).astype(jnp.bfloat16)
    suffix_value_grad = jnp.concatenate(suffix_value_pieces, axis=1).astype(jnp.bfloat16)
    pooled = jnp.concatenate(prefix_key_pieces + prefix_value_pieces, axis=1)
    reduced = sample_reduce(pooled).astype(jnp.bfloat16)

    partner_weight = [sample_gather(half, 0) for half in partner_half]
    if sections == 4:
        states_above = [
            swap(states_low, "section", 1),
            states_across[0],
            swap(states_across[0], "section", 1),
        ]
    else:
        states_above = states_across
    reduced, partner_weight, states_above = tied(reduced, partner_weight, states_above)

    own_rows = reduced.shape[0] // tensors
    high, low = tensor // 2, tensor % 2
    by_owner = reduced.reshape(tensors // 2, 2, own_rows, 2, head_width)
    keep = lax.dynamic_index_in_dim(by_owner, low, 1, False)
    give = lax.dynamic_index_in_dim(by_owner, 1 - low, 1, False)
    partner = swap(give, "tensor", 1)
    here = lambda rows: lax.dynamic_index_in_dim(rows, high, 0, False)
    there = lambda rows: lax.dynamic_index_in_dim(rows, 1 - high, 0, False)

    gain_wide = norm_gain[0].astype(jnp.float32)[None, :]
    states = states_low.astype(jnp.float32)
    inv_rms = lax.rsqrt(jnp.mean(states * states, axis=1, keepdims=True) + EPSILON)

    def partner_product(rows, chunk):
        pieces = times_weight(rows, partner_weight[chunk])
        if samples != 2:
            return pieces
        turned = jnp.concatenate([pieces[..., piece:], pieces[..., :piece]], axis=-1)
        return jnp.where(sample == 0, pieces, turned)

    owns = [weight[chunk * step : (chunk + 1) * step] for chunk in range(CHUNKS)]
    local, sent, theirs = {}, {}, {}
    for chunk in range(AHEAD, CHUNKS):
        theirs[chunk] = swap(
            times_weight(give, owns[chunk]).astype(jnp.bfloat16), "tensor", 1
        )
    for chunk in range(AHEAD):
        total = times_weight(keep, owns[chunk]) + partner_product(partner, chunk)
        sent[chunk] = swap(there(total).astype(jnp.bfloat16), "tensor", 2)
        local[chunk] = here(total)
    for chunk in range(AHEAD, CHUNKS):
        total = times_weight(keep, owns[chunk]) + theirs[chunk].astype(jnp.float32)
        sent[chunk] = swap(there(total).astype(jnp.bfloat16), "tensor", 2)
        local[chunk] = here(total)

    home = lax.all_to_all(
        reduced.reshape(-1, 2, head_width), "tensor", split_axis=0, concat_axis=2, tiled=True
    ).astype(jnp.float32)
    last = CHUNKS - 1
    sent[last], home, query_grad, rollout_key_gradient, suffix_value_grad = tied(
        sent[last], home, query_grad, rollout_key_gradient, suffix_value_grad
    )

    sums, along = [], 0.0
    for chunk in range(CHUNKS):
        cols = slice(chunk * step, (chunk + 1) * step)
        normed = local[chunk] + sent[chunk].astype(jnp.float32)
        gained = gain_wide[:, cols] * normed
        along = along + jnp.sum(states[:, cols] * gained, axis=1)
        sums.append(suffix_sum(inv_rms * gained))
    slope = inv_rms[:, 0] ** 3 * (along / width)
    state_part = states * slope[:, None]
    if sections == 4:
        peer = swap(slope, "section", 1)
        across = lax.ppermute(slope, "section", [(2, 0), (3, 1)])
        across_peer = lax.ppermute(slope, "section", [(2, 1), (3, 0)])
        odd = lax.axis_index("section") % 2 == 1
        slopes_above = [jnp.where(odd, 0.0, peer), across, across_peer]
    else:
        slopes_above = [from_above(slope, hop) for hop in range(1, sections)]
    for above, slope_above in zip(states_above, slopes_above):
        state_part = state_part + above.astype(jnp.float32) * slope_above[:, None]
    prefix_state_gradient = jnp.concatenate(sums, axis=1) - state_part

    return (
        query_grad[None],
        rollout_key_gradient[None],
        suffix_value_grad[None],
        home[:, 0][None],
        home[:, 1][None],
        prefix_state_gradient[None],
    )


def solution(mesh):
    placed = (
        P("section", "sample", "tensor"),
        P("section", "sample", "tensor"),
        P("section", "sample", "tensor"),
        P("section", "sample", "tensor"),
        P("section", ("sample", "tensor"), None),
        P("section", ("sample", "tensor"), None),
        P("section", None, None, "tensor"),
        P("section", ("sample", "tensor"), None),
        P("section", None),
        P("sample", None),
        P("sample", None),
        P(),
    )
    return jax.shard_map(
        on_device,
        mesh=mesh,
        in_specs=placed,
        out_specs=(
            P("section", "sample", "tensor"),
            P("section", "sample", "tensor"),
            P("section", "sample", "tensor"),
            P("section", ("sample", "tensor"), None),
            P("section", ("sample", "tensor"), None),
            P("section", ("sample", "tensor"), None),
        ),
        check_vma=False,
    )
```

```python
import jax
import jax.numpy as jnp
from jax import lax
from jax.sharding import PartitionSpec as P

HEAD_SIZE = 128
PAGE = 128


MASKED_SCORE = -1e30
EPSILON = 1e-05
CHUNKS = 4
LOADS = 2


def visible_keys(seg_row, prompt_row, table, page_ids):
    tok_count = seg_row.shape[0]
    seg_hot = seg_row[:, None] == jnp.arange(prompt_row.shape[0], dtype=jnp.int32)[None, :]
    prompt_tok = jnp.sum(jnp.where(seg_hot, prompt_row[None, :], 0), axis=1)
    member = jnp.any(table[:, :, None] == page_ids[None, None, :], axis=1)
    prompt_hot = prompt_tok[:, None] == jnp.arange(table.shape[0], dtype=jnp.int32)[None, :]
    member_tok = jnp.any(prompt_hot[:, :, None] & member[None, :, :], axis=1)
    prefix_seen = jnp.repeat(member_tok, PAGE, axis=1)
    position = jnp.arange(tok_count, dtype=jnp.int32)
    suffix_seen = (seg_row[:, None] == seg_row[None, :]) & (position[None, :] <= position[:, None])
    return jnp.concatenate([prefix_seen, suffix_seen], axis=1)


def attend_group(query_grp, grad_grp, key_rows, value_rows, visible):
    inv_root = query_grp.shape[-1] ** (-0.5)
    scores = (
        jnp.einsum("rgd,kd->rgk", query_grp, key_rows, preferred_element_type=jnp.float32)
        * inv_root
    )
    scores = jnp.where(visible[:, None, :], scores, MASKED_SCORE)
    row_max = jnp.max(scores, axis=2, keepdims=True)
    exponent = jnp.exp(scores - row_max)
    softmax_w = exponent / jnp.sum(exponent, axis=2, keepdims=True)
    weights_low = softmax_w.astype(jnp.bfloat16)
    attended = jnp.einsum(
        "rgk,kd->rgd", weights_low, value_rows, preferred_element_type=jnp.float32
    )
    delta_row = jnp.sum(grad_grp.astype(jnp.float32) * attended, axis=2, keepdims=True)
    weight_grad = jnp.einsum(
        "rgd,kd->rgk", grad_grp, value_rows, preferred_element_type=jnp.float32
    )
    score_grad = (softmax_w * (weight_grad - delta_row)).astype(jnp.bfloat16)
    query_out = (
        jnp.einsum("rgk,kd->rgd", score_grad, key_rows, preferred_element_type=jnp.float32)
        * inv_root
    )
    key_result = (
        jnp.einsum("rgk,rgd->kd", score_grad, query_grp, preferred_element_type=jnp.float32)
        * inv_root
    )
    value_out = jnp.einsum("rgk,rgd->kd", weights_low, grad_grp, preferred_element_type=jnp.float32)
    return (query_out, key_result, value_out)


def swap(value, axis, bit):
    count = lax.axis_size(axis)
    return lax.ppermute(value, axis, [(i, i ^ bit) for i in range(count)])


def sample_gather(value, axis):
    if lax.axis_size("sample") == 2:
        return jnp.concatenate([value, swap(value, "sample", 1)], axis=axis)
    return lax.all_gather(value, "sample", axis=axis, tiled=True)


def sample_sum(value):
    low = value.astype(jnp.bfloat16)
    if lax.axis_size("sample") == 2:
        half = value.shape[0] // 2
        theirs = swap(low, "sample", 1)
        theirs = jnp.concatenate([theirs[half:], theirs[:half]], axis=0)
        return (value + theirs.astype(jnp.float32)).astype(jnp.bfloat16)
    return lax.psum(low, "sample")


def times_weight(rows, weight):
    last = rows.ndim - 1
    return lax.dot_general(
        rows, weight, (((last - 1, last), (1, 2)), ((), ())), preferred_element_type=jnp.float32
    )


def tied(*values):
    return lax.optimization_barrier(values)


def suffix_all(term):
    count = lax.axis_size("section")
    gathered = lax.all_gather(term.astype(jnp.bfloat16), "section").astype(jnp.float32)
    above = (jnp.arange(count) > lax.axis_index("section"))[:, None, None]
    return term + jnp.sum(jnp.where(above, gathered, 0.0), axis=0)


def from_above(value, step):
    count = lax.axis_size("section")
    return lax.ppermute(value, "section", [(i, i - step) for i in range(step, count)])


def on_device(
    queries,
    suffix_keys,
    suffix_values,
    output_grad,
    prefix_keys,
    prefix_values,
    kv_weight,
    prefix_states,
    norm_gain,
    segment_ids,
    segment_prompt,
    block_table,
):
    head_width = suffix_keys.shape[2]
    samples = lax.axis_size("sample")
    sample = lax.axis_index("sample")
    tensors = lax.axis_size("tensor")
    tensor = lax.axis_index("tensor")
    sections = lax.axis_size("section")

    pool_own = jnp.concatenate([prefix_keys, prefix_values], axis=0)
    pool_mine = lax.all_to_all(pool_own, "tensor", split_axis=2, concat_axis=1, tiled=True)
    pool = sample_gather(pool_mine, 1)
    key_pool, value_pool = pool[0], pool[1]
    pooled_rows = key_pool.shape[0]
    pages = pooled_rows // PAGE
    page_ids = jnp.arange(pages, dtype=jnp.int32)
    if samples == 2:
        page_ids = (page_ids + sample.astype(jnp.int32) * (pages // 2)) % pages

    weight = kv_weight[0]
    width = weight.shape[0]
    share = width // samples
    piece = share // CHUNKS
    load = share // LOADS
    owns = [
        lax.dynamic_slice_in_dim(weight, sample * share + part * load, load, 0)
        for part in range(LOADS)
    ]
    partner_weight = [swap(own, "tensor", 1) for own in owns]
    early = LOADS // 2

    def chunk_of(parts, chunk):
        held = CHUNKS // LOADS
        first = chunk % held * piece
        return parts[chunk // held][first : first + piece]

    states_low = prefix_states[0]
    if sections == 4:
        states_across = [lax.ppermute(states_low, "section", [(2, 0), (3, 1)])]
    else:
        states_across = [from_above(states_low, hop) for hop in range(1, sections)]

    tok_count = queries.shape[1]
    kv_local = head_width // HEAD_SIZE
    group_size = queries.shape[2] // head_width
    visible = visible_keys(segment_ids[0], segment_prompt[0], block_table, page_ids)
    query_rows = queries[0].reshape(tok_count, kv_local, group_size, HEAD_SIZE)
    grad_rows = output_grad[0].reshape(tok_count, kv_local, group_size, HEAD_SIZE)
    own_keys = suffix_keys[0]
    own_values = suffix_values[0]
    high, low = tensor // 2, tensor % 2
    own_rows = pooled_rows // samples // tensors
    query_pieces, suffix_key_pieces, suffix_value_pieces = [], [], []
    full_pieces, keep_pieces, partner_pieces = [], [], []
    for head_index in range(kv_local):
        low_col = head_index * HEAD_SIZE
        cols = slice(low_col, low_col + HEAD_SIZE)
        if head_index == 1:
            key_pool, value_pool, partner_weight[:early], states_across = tied(
                key_pool, value_pool, partner_weight[:early], states_across
            )
        key_rows = jnp.concatenate([key_pool[:, cols], own_keys[:, cols]], axis=0)
        value_rows = jnp.concatenate([value_pool[:, cols], own_values[:, cols]], axis=0)
        query_out, key_result, value_out = attend_group(
            query_rows[:, head_index], grad_rows[:, head_index], key_rows, value_rows, visible
        )
        query_pieces.append(query_out)
        suffix_key_pieces.append(key_result[pooled_rows:])
        suffix_value_pieces.append(value_out[pooled_rows:])
        pooled = jnp.concatenate([key_result[:pooled_rows], value_out[:pooled_rows]], axis=1)
        full = sample_sum(pooled)
        by_owner = full.reshape(samples, tensors // 2, 2, own_rows, 2, HEAD_SIZE)
        full_pieces.append(by_owner)
        keep_pieces.append(lax.dynamic_index_in_dim(by_owner, low, 2, False))
        give = lax.dynamic_index_in_dim(by_owner, 1 - low, 2, False)
        partner_pieces.append(swap(give, "tensor", 1))
    query_grad = jnp.stack(query_pieces, axis=1).reshape(tok_count, -1).astype(jnp.bfloat16)
    rollout_key_gradient = jnp.concatenate(suffix_key_pieces, axis=1).astype(jnp.bfloat16)
    suffix_value_grad = jnp.concatenate(suffix_value_pieces, axis=1).astype(jnp.bfloat16)
    if sections == 4:
        states_above = [
            swap(states_low, "section", 1),
            states_across[0],
            swap(states_across[0], "section", 1),
        ]
    else:
        states_above = states_across
    partner_pieces, partner_weight, states_above = tied(
        partner_pieces, partner_weight, states_above
    )
    keep = jnp.concatenate(keep_pieces, axis=-1)
    partner = jnp.concatenate(partner_pieces, axis=-1)
    full = jnp.concatenate(full_pieces, axis=-1)
    at_home = 0 if samples == 2 else sample
    reduced = lax.dynamic_index_in_dim(full, at_home, 0, False).reshape(-1, 2, head_width)
    here = lambda rows: lax.dynamic_index_in_dim(rows, high, 1, False)
    there = lambda rows: lax.dynamic_index_in_dim(rows, 1 - high, 1, False)

    gain_wide = norm_gain[0].astype(jnp.float32)[None, :]
    states = states_low.astype(jnp.float32)
    inv_rms = lax.rsqrt(jnp.mean(states * states, axis=1, keepdims=True) + EPSILON)

    keep_here, keep_there = here(keep), there(keep)
    partner_here, partner_there = here(partner), there(partner)
    local, sent = [], []
    for chunk in range(CHUNKS):
        total = times_weight(keep_there, chunk_of(owns, chunk)) + times_weight(
            partner_there, chunk_of(partner_weight, chunk)
        )
        sent.append(swap(total.astype(jnp.bfloat16), "tensor", 2))
    for chunk in range(CHUNKS):
        local.append(
            times_weight(keep_here, chunk_of(owns, chunk))
            + times_weight(partner_here, chunk_of(partner_weight, chunk))
        )

    home = lax.all_to_all(
        reduced, "tensor", split_axis=0, concat_axis=2, tiled=True
    ).astype(jnp.float32)
    last = CHUNKS - 1
    sent[last], home, query_grad, rollout_key_gradient, suffix_value_grad = tied(
        sent[last], home, query_grad, rollout_key_gradient, suffix_value_grad
    )

    odd = lax.axis_index("section") % 2 == 1

    def of_chunk(rows, chunk):
        parts = rows.reshape(rows.shape[0], samples, CHUNKS, piece)
        return parts[:, :, chunk].reshape(rows.shape[0], samples * piece)

    def to_samples(chunk, arrived):
        normed = local[chunk] + arrived.astype(jnp.float32)
        if samples == 2:
            return normed[0], swap(normed[1].astype(jnp.bfloat16), "sample", 1)
        return None, lax.all_to_all(normed.astype(jnp.bfloat16), "sample", 0, 0, tiled=True)

    def whole_chunk(mine, arrived):
        arrived = arrived.astype(jnp.float32)
        if samples == 2:
            return jnp.where(
                sample == 0,
                jnp.concatenate([mine, arrived], axis=1),
                jnp.concatenate([arrived, mine], axis=1),
            )
        return jnp.concatenate([arrived[i] for i in range(samples)], axis=1)

    sums, along = [None] * CHUNKS, 0.0
    mine, at_sample, terms, at_core = {}, {}, {}, {}
    peers, at_across, at_back, got = {}, {}, {}, {}
    for tick in range(CHUNKS + 4):
        if tick < CHUNKS:
            waiting = [
                (held, tick - 1 - place)
                for place, held in enumerate((at_sample, at_core, at_across, at_back))
                if tick - 1 - place in held
            ]
            sent[tick], ready = tied(sent[tick], [held[key] for held, key in waiting])
            for (held, key), value in zip(waiting, ready):
                held[key] = value
        chunk = tick - 4
        if chunk >= 0 and sections == 4:
            upper = jnp.where(
                odd,
                jnp.concatenate([at_back[chunk], got[chunk]], axis=1),
                jnp.concatenate([got[chunk], at_back[chunk]], axis=1),
            )
            below = terms[chunk] + jnp.where(odd, 0.0, peers[chunk])
            sums[chunk] = below + upper.astype(jnp.float32)
        chunk = tick - 3
        if 0 <= chunk < CHUNKS and sections == 4:
            got[chunk] = at_across[chunk]
            at_back[chunk] = lax.ppermute(got[chunk], "section", [(0, 1), (1, 0)])
        chunk = tick - 2
        if 0 <= chunk < CHUNKS and sections == 4:
            peers[chunk] = at_core[chunk].astype(jnp.float32)
            pair = (terms[chunk] + peers[chunk]).astype(jnp.bfloat16)
            half = pair.shape[1] // 2
            part = jnp.where(odd, pair[:, half:], pair[:, :half])
            at_across[chunk] = lax.ppermute(part, "section", [(2, 0), (3, 1)])
        chunk = tick - 1
        if 0 <= chunk < CHUNKS:
            gained = of_chunk(gain_wide, chunk) * whole_chunk(mine[chunk], at_sample[chunk])
            along = along + jnp.sum(of_chunk(states, chunk) * gained, axis=1)
            terms[chunk] = inv_rms * gained
            if sections == 4:
                at_core[chunk] = swap(terms[chunk].astype(jnp.bfloat16), "section", 1)
            else:
                sums[chunk] = suffix_all(terms[chunk])
        if tick < CHUNKS:
            mine[tick], at_sample[tick] = to_samples(tick, sent[tick])
    slope = inv_rms[:, 0] ** 3 * (along / width)
    state_part = states * slope[:, None]
    if sections == 4:
        peer = swap(slope, "section", 1)
        across = lax.ppermute(slope, "section", [(2, 0), (3, 1)])
        across_peer = lax.ppermute(slope, "section", [(2, 1), (3, 0)])
        slopes_above = [jnp.where(odd, 0.0, peer), across, across_peer]
    else:
        slopes_above = [from_above(slope, hop) for hop in range(1, sections)]
    for above, slope_above in zip(states_above, slopes_above):
        state_part = state_part + above.astype(jnp.float32) * slope_above[:, None]
    ordered = [
        sums[chunk][:, part * piece : (part + 1) * piece]
        for part in range(samples)
        for chunk in range(CHUNKS)
    ]
    prefix_state_gradient = jnp.concatenate(ordered, axis=1) - state_part

    return (
        query_grad[None],
        rollout_key_gradient[None],
        suffix_value_grad[None],
        home[:, 0][None],
        home[:, 1][None],
        prefix_state_gradient[None],
    )


def solution(mesh):
    placed = (
        P("section", "sample", "tensor"),
        P("section", "sample", "tensor"),
        P("section", "sample", "tensor"),
        P("section", "sample", "tensor"),
        P("section", ("sample", "tensor"), None),
        P("section", ("sample", "tensor"), None),
        P("section", None, None, "tensor"),
        P("section", ("sample", "tensor"), None),
        P("section", None),
        P("sample", None),
        P("sample", None),
        P(),
    )
    return jax.shard_map(
        on_device,
        mesh=mesh,
        in_specs=placed,
        out_specs=(
            P("section", "sample", "tensor"),
            P("section", "sample", "tensor"),
            P("section", "sample", "tensor"),
            P("section", ("sample", "tensor"), None),
            P("section", ("sample", "tensor"), None),
            P("section", ("sample", "tensor"), None),
        ),
        check_vma=False,
    )
```

```python
import jax
import jax.numpy as jnp
from jax import lax
from jax.sharding import PartitionSpec as P

HEAD_SIZE = 128
PAGE = 128


MASKED_SCORE = -1e30
EPSILON = 1e-05
CHUNKS = 2
LOADS = 2


def visible_keys(seg_row, prompt_row, table, page_ids):
    tok_count = seg_row.shape[0]
    seg_hot = seg_row[:, None] == jnp.arange(prompt_row.shape[0], dtype=jnp.int32)[None, :]
    prompt_tok = jnp.sum(jnp.where(seg_hot, prompt_row[None, :], 0), axis=1)
    member = jnp.any(table[:, :, None] == page_ids[None, None, :], axis=1)
    prompt_hot = prompt_tok[:, None] == jnp.arange(table.shape[0], dtype=jnp.int32)[None, :]
    member_tok = jnp.any(prompt_hot[:, :, None] & member[None, :, :], axis=1)
    prefix_seen = jnp.repeat(member_tok, PAGE, axis=1)
    position = jnp.arange(tok_count, dtype=jnp.int32)
    suffix_seen = (seg_row[:, None] == seg_row[None, :]) & (position[None, :] <= position[:, None])
    return jnp.concatenate([prefix_seen, suffix_seen], axis=1)


def attend_group(query_grp, grad_grp, key_rows, value_rows, visible):
    inv_root = query_grp.shape[-1] ** (-0.5)
    scores = (
        jnp.einsum("rgd,kd->rgk", query_grp, key_rows, preferred_element_type=jnp.float32)
        * inv_root
    )
    scores = jnp.where(visible[:, None, :], scores, MASKED_SCORE)
    row_max = jnp.max(scores, axis=2, keepdims=True)
    exponent = jnp.exp(scores - row_max)
    softmax_w = exponent / jnp.sum(exponent, axis=2, keepdims=True)
    weights_low = softmax_w.astype(jnp.bfloat16)
    attended = jnp.einsum(
        "rgk,kd->rgd", weights_low, value_rows, preferred_element_type=jnp.float32
    )
    delta_row = jnp.sum(grad_grp.astype(jnp.float32) * attended, axis=2, keepdims=True)
    weight_grad = jnp.einsum(
        "rgd,kd->rgk", grad_grp, value_rows, preferred_element_type=jnp.float32
    )
    score_grad = (softmax_w * (weight_grad - delta_row)).astype(jnp.bfloat16)
    query_out = (
        jnp.einsum("rgk,kd->rgd", score_grad, key_rows, preferred_element_type=jnp.float32)
        * inv_root
    )
    key_result = (
        jnp.einsum("rgk,rgd->kd", score_grad, query_grp, preferred_element_type=jnp.float32)
        * inv_root
    )
    value_out = jnp.einsum("rgk,rgd->kd", weights_low, grad_grp, preferred_element_type=jnp.float32)
    return (query_out, key_result, value_out)


def swap(value, axis, bit):
    count = lax.axis_size(axis)
    return lax.ppermute(value, axis, [(i, i ^ bit) for i in range(count)])


def sample_gather(value, axis):
    if lax.axis_size("sample") == 2:
        return jnp.concatenate([value, swap(value, "sample", 1)], axis=axis)
    return lax.all_gather(value, "sample", axis=axis, tiled=True)


def sample_sum(value):
    low = value.astype(jnp.bfloat16)
    if lax.axis_size("sample") == 2:
        half = value.shape[0] // 2
        theirs = swap(low, "sample", 1)
        theirs = jnp.concatenate([theirs[half:], theirs[:half]], axis=0)
        return (value + theirs.astype(jnp.float32)).astype(jnp.bfloat16)
    return lax.psum(low, "sample")


def times_weight(rows, weight):
    last = rows.ndim - 1
    return lax.dot_general(
        rows, weight, (((last - 1, last), (1, 2)), ((), ())), preferred_element_type=jnp.float32
    )


def tied(*values):
    return lax.optimization_barrier(values)


def suffix_all(term):
    count = lax.axis_size("section")
    gathered = lax.all_gather(term.astype(jnp.bfloat16), "section").astype(jnp.float32)
    above = (jnp.arange(count) > lax.axis_index("section"))[:, None, None]
    return term + jnp.sum(jnp.where(above, gathered, 0.0), axis=0)


def from_above(value, step):
    count = lax.axis_size("section")
    return lax.ppermute(value, "section", [(i, i - step) for i in range(step, count)])


def on_device(
    queries,
    suffix_keys,
    suffix_values,
    output_grad,
    prefix_keys,
    prefix_values,
    kv_weight,
    prefix_states,
    norm_gain,
    segment_ids,
    segment_prompt,
    block_table,
):
    head_width = suffix_keys.shape[2]
    samples = lax.axis_size("sample")
    sample = lax.axis_index("sample")
    tensors = lax.axis_size("tensor")
    tensor = lax.axis_index("tensor")
    sections = lax.axis_size("section")

    pool_own = jnp.concatenate([prefix_keys, prefix_values], axis=0)
    pool_mine = lax.all_to_all(pool_own, "tensor", split_axis=2, concat_axis=1, tiled=True)
    pool = sample_gather(pool_mine, 1)
    key_pool, value_pool = pool[0], pool[1]
    pooled_rows = key_pool.shape[0]
    pages = pooled_rows // PAGE
    page_ids = jnp.arange(pages, dtype=jnp.int32)
    if samples == 2:
        page_ids = (page_ids + sample.astype(jnp.int32) * (pages // 2)) % pages

    weight = kv_weight[0]
    width = weight.shape[0]
    share = width // samples
    piece = share // CHUNKS
    load = share // LOADS
    owns = [
        lax.dynamic_slice_in_dim(weight, sample * share + part * load, load, 0)
        for part in range(LOADS)
    ]
    partner_weight = [swap(own, "tensor", 1) for own in owns]
    early = LOADS // 2

    def chunk_of(parts, chunk):
        held = CHUNKS // LOADS
        first = chunk % held * piece
        return parts[chunk // held][first : first + piece]

    states_low = prefix_states[0]
    if sections == 4:
        states_across = [lax.ppermute(states_low, "section", [(2, 0), (3, 1)])]
    else:
        states_across = [from_above(states_low, hop) for hop in range(1, sections)]

    tok_count = queries.shape[1]
    kv_local = head_width // HEAD_SIZE
    group_size = queries.shape[2] // head_width
    visible = visible_keys(segment_ids[0], segment_prompt[0], block_table, page_ids)
    query_rows = queries[0].reshape(tok_count, kv_local, group_size, HEAD_SIZE)
    grad_rows = output_grad[0].reshape(tok_count, kv_local, group_size, HEAD_SIZE)
    own_keys = suffix_keys[0]
    own_values = suffix_values[0]
    high, low = tensor // 2, tensor % 2
    own_rows = pooled_rows // samples // tensors
    query_pieces, suffix_key_pieces, suffix_value_pieces = [], [], []
    full_pieces, keep_pieces, partner_pieces = [], [], []
    for head_index in range(kv_local):
        low_col = head_index * HEAD_SIZE
        cols = slice(low_col, low_col + HEAD_SIZE)
        if head_index == 1:
            key_pool, value_pool, partner_weight[:early], states_across = tied(
                key_pool, value_pool, partner_weight[:early], states_across
            )
        key_rows = jnp.concatenate([key_pool[:, cols], own_keys[:, cols]], axis=0)
        value_rows = jnp.concatenate([value_pool[:, cols], own_values[:, cols]], axis=0)
        query_out, key_result, value_out = attend_group(
            query_rows[:, head_index], grad_rows[:, head_index], key_rows, value_rows, visible
        )
        query_pieces.append(query_out)
        suffix_key_pieces.append(key_result[pooled_rows:])
        suffix_value_pieces.append(value_out[pooled_rows:])
        pooled = jnp.concatenate([key_result[:pooled_rows], value_out[:pooled_rows]], axis=1)
        full = sample_sum(pooled)
        by_owner = full.reshape(samples, tensors // 2, 2, own_rows, 2, HEAD_SIZE)
        full_pieces.append(by_owner)
        keep_pieces.append(lax.dynamic_index_in_dim(by_owner, low, 2, False))
        give = lax.dynamic_index_in_dim(by_owner, 1 - low, 2, False)
        partner_pieces.append(swap(give, "tensor", 1))
    query_grad = jnp.stack(query_pieces, axis=1).reshape(tok_count, -1).astype(jnp.bfloat16)
    rollout_key_gradient = jnp.concatenate(suffix_key_pieces, axis=1).astype(jnp.bfloat16)
    suffix_value_grad = jnp.concatenate(suffix_value_pieces, axis=1).astype(jnp.bfloat16)
    if sections == 4:
        states_above = [
            swap(states_low, "section", 1),
            states_across[0],
            swap(states_across[0], "section", 1),
        ]
    else:
        states_above = states_across
    partner_pieces, partner_weight, states_above = tied(
        partner_pieces, partner_weight, states_above
    )
    keep = jnp.concatenate(keep_pieces, axis=-1)
    partner = jnp.concatenate(partner_pieces, axis=-1)
    full = jnp.concatenate(full_pieces, axis=-1)
    at_home = 0 if samples == 2 else sample
    reduced = lax.dynamic_index_in_dim(full, at_home, 0, False).reshape(-1, 2, head_width)
    here = lambda rows: lax.dynamic_index_in_dim(rows, high, 1, False)
    there = lambda rows: lax.dynamic_index_in_dim(rows, 1 - high, 1, False)

    gain_wide = norm_gain[0].astype(jnp.float32)[None, :]
    states = states_low.astype(jnp.float32)
    inv_rms = lax.rsqrt(jnp.mean(states * states, axis=1, keepdims=True) + EPSILON)

    keep_here, keep_there = here(keep), there(keep)
    partner_here, partner_there = here(partner), there(partner)
    local, sent = [], []
    for chunk in range(CHUNKS):
        total = times_weight(keep_there, chunk_of(owns, chunk)) + times_weight(
            partner_there, chunk_of(partner_weight, chunk)
        )
        total = total.astype(jnp.bfloat16)
        if chunk:
            total, sent[chunk - 1] = tied(total, sent[chunk - 1])
        sent.append(swap(total, "tensor", 2))
    for chunk in range(CHUNKS):
        local.append(
            times_weight(keep_here, chunk_of(owns, chunk))
            + times_weight(partner_here, chunk_of(partner_weight, chunk))
        )

    home = lax.all_to_all(
        reduced, "tensor", split_axis=0, concat_axis=2, tiled=True
    ).astype(jnp.float32)
    last = CHUNKS - 1
    sent[last], home, query_grad, rollout_key_gradient, suffix_value_grad = tied(
        sent[last], home, query_grad, rollout_key_gradient, suffix_value_grad
    )

    odd = lax.axis_index("section") % 2 == 1

    def of_chunk(rows, chunk):
        starts = [part * share + chunk * piece for part in range(samples)]
        return jnp.concatenate([rows[:, start : start + piece] for start in starts], axis=1)

    def to_samples(chunk, arrived):
        normed = local[chunk] + arrived.astype(jnp.float32)
        if samples == 2:
            return normed[0], swap(normed[1].astype(jnp.bfloat16), "sample", 1)
        return None, lax.all_to_all(normed.astype(jnp.bfloat16), "sample", 0, 0, tiled=True)

    def whole_chunk(mine, arrived):
        arrived = arrived.astype(jnp.float32)
        if samples == 2:
            return jnp.where(
                sample == 0,
                jnp.concatenate([mine, arrived], axis=1),
                jnp.concatenate([arrived, mine], axis=1),
            )
        return jnp.concatenate([arrived[i] for i in range(samples)], axis=1)

    sums, along = [None] * CHUNKS, 0.0
    mine, at_sample, terms, at_core = {}, {}, {}, {}
    peers, at_across, at_back, got = {}, {}, {}, {}
    for tick in range(CHUNKS + 4):
        if tick < CHUNKS:
            waiting = [
                (held, tick - 1 - place)
                for place, held in enumerate((at_sample, at_core, at_across, at_back))
                if tick - 1 - place in held
            ]
            sent[tick], ready = tied(sent[tick], [held[key] for held, key in waiting])
            for (held, key), value in zip(waiting, ready):
                held[key] = value
        chunk = tick - 4
        if chunk >= 0 and sections == 4:
            upper = jnp.where(
                odd,
                jnp.concatenate([at_back[chunk], got[chunk]], axis=1),
                jnp.concatenate([got[chunk], at_back[chunk]], axis=1),
            )
            below = terms[chunk] + jnp.where(odd, 0.0, peers[chunk])
            sums[chunk] = below + upper.astype(jnp.float32)
        chunk = tick - 3
        if 0 <= chunk < CHUNKS and sections == 4:
            got[chunk] = at_across[chunk]
            at_back[chunk] = lax.ppermute(got[chunk], "section", [(0, 1), (1, 0)])
        chunk = tick - 2
        if 0 <= chunk < CHUNKS and sections == 4:
            peers[chunk] = at_core[chunk].astype(jnp.float32)
            pair = (terms[chunk] + peers[chunk]).astype(jnp.bfloat16)
            half = pair.shape[1] // 2
            part = jnp.where(odd, pair[:, half:], pair[:, :half])
            at_across[chunk] = lax.ppermute(part, "section", [(2, 0), (3, 1)])
        chunk = tick - 1
        if 0 <= chunk < CHUNKS:
            gained = of_chunk(gain_wide, chunk) * whole_chunk(mine[chunk], at_sample[chunk])
            along = along + jnp.sum(of_chunk(states, chunk) * gained, axis=1)
            terms[chunk] = inv_rms * gained
            if sections == 4:
                at_core[chunk] = swap(terms[chunk].astype(jnp.bfloat16), "section", 1)
            else:
                sums[chunk] = suffix_all(terms[chunk])
        if tick < CHUNKS:
            mine[tick], at_sample[tick] = to_samples(tick, sent[tick])
    slope = inv_rms[:, 0] ** 3 * (along / width)
    state_part = states * slope[:, None]
    if sections == 4:
        peer = swap(slope, "section", 1)
        across = lax.ppermute(slope, "section", [(2, 0), (3, 1)])
        across_peer = lax.ppermute(slope, "section", [(2, 1), (3, 0)])
        slopes_above = [jnp.where(odd, 0.0, peer), across, across_peer]
    else:
        slopes_above = [from_above(slope, hop) for hop in range(1, sections)]
    for above, slope_above in zip(states_above, slopes_above):
        state_part = state_part + above.astype(jnp.float32) * slope_above[:, None]
    ordered = [
        sums[chunk][:, part * piece : (part + 1) * piece]
        for part in range(samples)
        for chunk in range(CHUNKS)
    ]
    prefix_state_gradient = jnp.concatenate(ordered, axis=1) - state_part

    return (
        query_grad[None],
        rollout_key_gradient[None],
        suffix_value_grad[None],
        home[:, 0][None],
        home[:, 1][None],
        prefix_state_gradient[None],
    )


def solution(mesh):
    placed = (
        P("section", "sample", "tensor"),
        P("section", "sample", "tensor"),
        P("section", "sample", "tensor"),
        P("section", "sample", "tensor"),
        P("section", ("sample", "tensor"), None),
        P("section", ("sample", "tensor"), None),
        P("section", None, None, "tensor"),
        P("section", ("sample", "tensor"), None),
        P("section", None),
        P("sample", None),
        P("sample", None),
        P(),
    )
    return jax.shard_map(
        on_device,
        mesh=mesh,
        in_specs=placed,
        out_specs=(
            P("section", "sample", "tensor"),
            P("section", "sample", "tensor"),
            P("section", "sample", "tensor"),
            P("section", ("sample", "tensor"), None),
            P("section", ("sample", "tensor"), None),
            P("section", ("sample", "tensor"), None),
        ),
        check_vma=False,
    )
```
